32 devices in a mesh: snap: 2 (over y), gx: 8 (over z, x), gy: 2 (over core).
Axes of the slice: x: 2, y: 2, z: 4, core: 2. Of those that a mesh axis runs over, the one named last changes fastest.
Arguments:
- snapshot: float32 [32, 256, 12, 128], P(('snap', 'gx'), 'gy'), parts along dimension 0, may hold values from -64 to 64
- factor_x: float32 [16, 64], P('gx')
- factor_y: float32 [256, 64], P(None, 'gy')
- factor_var: float32 [12, 4], replicated
Outputs:
- gram: float32 [256, 128], P('snap'), parts along dimension 0
The draws below stay inside these ranges and needn't reach their ends.
There are 2 independent parts, one for each index of `snap`. The reference program is written for one: setup_inputs(seed, part) draws one part's arguments, and reference() takes and returns one part's arrays. A program takes and returns all parts, laid end to end along the dimension named above; an argument that names none is the same for every part. Nothing has to cross between parts.
All inputs are finite; a program needn't handle non-finite values.
Results may differ from the reference program's by a relative error of at most 0.000087.
Values sent between devices are 32-bit elements; how exact they have to be, the bound alone decides.
A program may use at most 64 MiB of HBM per device.

```python
import math
import jax
import jax.numpy as jnp
from jax import lax

NZ = 128
NV = 12
RX = 64
RY = 64
RV = 4
NX = 16
NY = 256


def scale_columns(key, entries, spread):
    columns = entries.shape[1]
    factors = jnp.exp(jax.random.uniform(key, (columns,), jnp.float32, -math.log(spread), math.log(spread)))
    return entries * factors[None, :] * entries.shape[0] ** (-0.5)


def draw_snapshot(key, part):
    key = jax.random.fold_in(key, 11)
    keys = jax.random.split(key, 4)
    values = jax.random.truncated_normal(keys[0], -4.0, 4.0, (NX, NY, NV, NZ), jnp.float32)
    x_scale = jnp.exp(jax.random.uniform(keys[1], (NX,), jnp.float32, math.log(0.5), math.log(2.0)))
    var_scale = jnp.exp(jax.random.uniform(keys[2], (NV,), jnp.float32, math.log(0.1), math.log(2.0)))
    pairing = jax.random.permutation(keys[3], NZ)
    partner = pairing[jnp.arange(NX) % NZ]
    spike = jnp.where(jnp.arange(NZ)[None, :] == partner[:, None], 4.0, 1.0)
    return values * x_scale[:, None, None, None] * var_scale[None, None, :, None] * spike[:, None, None, :]


def draw_factor_x(key, part):
    key = jax.random.fold_in(key, 21)
    first, second = jax.random.split(key)
    entries = jax.random.truncated_normal(first, -4.0, 4.0, (NX, RX), jnp.float32)
    return scale_columns(second, entries, 2.0)


def draw_factor_y(key, part):
    key = jax.random.fold_in(key, 31)
    first, second = jax.random.split(key)
    entries = jax.random.truncated_normal(first, -4.0, 4.0, (NY, RY), jnp.float32)
    return scale_columns(second, entries, 2.0)


def draw_factor_var(key, part):
    key = jax.random.fold_in(key, 41)
    first, second = jax.random.split(key)
    entries = jax.random.truncated_normal(first, -4.0, 4.0, (NV, RV), jnp.float32)
    return scale_columns(second, entries, 2.0)


def setup_inputs(seed: int = 0, part: int = 0) -> dict:
    key_of = jax.random.split(jax.random.key(seed), 5)
    part_splits = jax.random.split(jax.random.fold_in(key_of[4], part), 5)
    snapshot = draw_snapshot(jax.random.fold_in(jax.random.fold_in(key_of[4], part), 71), part)
    factor_x = draw_factor_x(jax.random.fold_in(key_of[4], 71), part)
    factor_y = draw_factor_y(jax.random.fold_in(key_of[4], 71), part)
    factor_var = draw_factor_var(jax.random.fold_in(key_of[4], 71), part)
    return {"snapshot": snapshot, "factor_x": factor_x, "factor_y": factor_y, "factor_var": factor_var}


def reference(snapshot, factor_x, factor_y, factor_var):
    highest = lax.Precision.HIGHEST
    reduced = jnp.einsum('xyvz,vq->xyqz', snapshot, factor_var, precision=highest)
    contracted = jnp.einsum('xyqz,yp->xpqz', reduced, factor_y, precision=highest)
    projected = jnp.einsum('xpqz,xr->rpqz', contracted, factor_x, precision=highest)
    unfolded = projected.reshape(-1, NZ)
    summed = jnp.dot(unfolded.T, unfolded, precision=highest, preferred_element_type=jnp.float32)
    return summed * (1.0 / (RX * RY * RV))
```

```python
import functools

import jax
import jax.numpy as jnp
from jax import lax
from jax.experimental import pallas as pl
from jax.experimental.pallas import tpu as pltpu
from jax.sharding import PartitionSpec as P

MESH = pl.DeviceIdType.MESH
HIGHEST = lax.Precision.HIGHEST
CORES = 2
SUBLANES = 8


def dot(a, b, dims=((1,), (0,))):
    return lax.dot_general(a, b, (dims, ((), ())), precision=HIGHEST, preferred_element_type=jnp.float32)


def loop(first, last, body):
    def step(i, carry):
        body(i)
        return carry

    lax.fori_loop(first, last, step, 0, unroll=(last - first) <= 16)


def kernel(
    n_gx, scale,
    snap_ref, fx_ref, fyt_ref, fv_ref, out_ref,
    snap, reduced, fx_all, fy_send, fy_recv, half_send, half_recv, part, blocks, gram, pieces,
    snap_sem, fy_sems, fx_send, fx_recv, half_ssem, half_rsem, a2a_send, a2a_recv, rs_send, rs_recv, ag_send, ag_recv,
):
    gx, gy = lax.axis_index("gx"), lax.axis_index("gy")
    other = 1 - gy
    total = n_gx * CORES
    me = gx * CORES + gy
    local_x, n_var, local_y, depth = snap.shape
    n_q = reduced.shape[0]
    _, _, k, _ = blocks.shape
    per_q = n_gx // n_q
    owners = min(total, depth // SUBLANES)

    def device(t):
        return {"gx": t // CORES, "gy": t % CORES}

    def remote(src, dst, send, recv, where):
        return pltpu.make_async_remote_copy(
            src_ref=src, dst_ref=dst, send_sem=send, recv_sem=recv, device_id=where, device_id_type=MESH
        )

    loads = [pltpu.make_async_copy(snap_ref.at[x], snap.at[x], snap_sem.at[x]) for x in range(local_x)]
    for load in loads:
        load.start()

    barrier = pltpu.get_barrier_semaphore()
    loop(1, total, lambda s: pl.semaphore_signal(
        barrier, inc=1, device_id=device(lax.rem(me + s, total)), device_id_type=MESH))

    fx = fx_ref[...]
    rank = fx.shape[1]
    fx_wide = jnp.concatenate([fx, jnp.zeros((local_x, depth - rank), jnp.float32)], axis=1) if rank < depth else fx
    for x in range(local_x):
        fx_all[gx, x] = fx_wide[x : x + 1]
    fy_send[...] = fyt_ref[:, pl.ds(pl.multiple_of(other * local_y, local_y), local_y)]
    fy_mine = fyt_ref[:, pl.ds(pl.multiple_of(gy * local_y, local_y), local_y)]

    pl.semaphore_wait(barrier, total - 1)

    fy_copy = remote(fy_send, fy_recv, fy_sems.at[0], fy_sems.at[1], {"gy": other})
    fy_copy.start()

    def fx_copy(j):
        return remote(fx_all.at[gx], fx_all.at[gx], fx_send.at[j], fx_recv.at[gx], {"gx": j})

    loop(1, n_gx, lambda s: fx_copy(lax.rem(gx + s, n_gx)).start())

    rows = 16
    for x in range(local_x):
        loads[x].wait()

        def var_step(i, carry, x=x):
            at = pl.ds(pl.multiple_of(i * rows, rows), rows)
            sums = [None] * n_q
            for v in range(n_var):
                cells = snap[x, v, at, :]
                for q in range(n_q):
                    term = cells * fv_ref[v, q]
                    sums[q] = term if v == 0 else sums[q] + term
            for q in range(n_q):
                reduced[q, at, x * depth : (x + 1) * depth] = sums[q]
            return carry

        lax.fori_loop(0, local_y // rows, var_step, 0)

    def put(ref, q, value):
        for x in range(local_x):
            cells = value[:, x * depth : (x + 1) * depth]
            ref[q * per_q : (q + 1) * per_q, x] = cells.reshape(per_q, k, depth)

    fy_copy.wait_recv()
    fy_theirs = fy_recv[...]
    halves = []
    for q in range(n_q):
        put(half_send, q, dot(fy_theirs, reduced[q]))
        at = pl.ds(q * per_q, per_q)
        half = remote(half_send.at[at], half_recv.at[at], half_ssem.at[q], half_rsem.at[q], {"gy": other})
        half.start()
        halves.append(half)
    for q in range(n_q):
        put(part, q, dot(fy_mine, reduced[q]))

    def block_copy(j):
        return remote(part.at[j], blocks.at[gx], a2a_send.at[j], a2a_recv.at[gx], {"gx": j})

    for q in range(n_q):
        at = pl.ds(q * per_q, per_q)
        halves[q].wait_recv()
        part[at] = part[at] + half_recv[at]

        def send_block(j):
            @pl.when(j != gx)
            def _():
                block_copy(j).start()

        loop(q * per_q, (q + 1) * per_q, send_block)
    blocks[gx] = part[gx]

    def arrived(sems, ref, j):
        remote(ref.at[gx], ref.at[j], fx_send.at[j], sems.at[j], {"gx": j}).wait_recv()

    loop(1, n_gx, lambda s: arrived(fx_recv, fx_all, lax.rem(gx + s, n_gx)))
    wide = n_gx * local_x * k
    factor = jnp.broadcast_to(fx_all[...], (n_gx, local_x, k, depth)).reshape(wide, depth)
    largest = jnp.max(jnp.abs(factor), axis=1, keepdims=True)
    largest = jnp.where(largest > 0.0, largest, 1.0)
    unit = factor / largest
    same = (
        lax.broadcasted_iota(jnp.int32, (wide, wide), 0) % k
        == lax.broadcasted_iota(jnp.int32, (wide, wide), 1) % k
    )
    mixing = jnp.where(same, dot(unit, unit, ((1,), (1,))), 0.0)

    loop(1, n_gx, lambda s: arrived(a2a_recv, blocks, lax.rem(gx + s, n_gx)))
    cells = blocks[...].reshape(wide, depth) * largest
    gram[...] = dot(cells, dot(mixing, cells), ((0,), (0,)))

    def piece_copy(t):
        at = pl.ds(pl.multiple_of(t * SUBLANES, SUBLANES), SUBLANES)
        return remote(gram.at[at], pieces.at[me], rs_send.at[t], rs_recv.at[me], device(t))

    def row_copy(t):
        at = pl.ds(pl.multiple_of(me * SUBLANES, SUBLANES), SUBLANES)
        return remote(out_ref.at[at], out_ref.at[at], ag_send.at[t], ag_recv.at[me], device(t))

    def owned(t, body):
        if owners == total:
            body()
        else:
            pl.when(t < owners)(body)

    def others(body):
        loop(1, total, lambda s: body(lax.rem(me + s, total)))

    others(lambda t: owned(t, lambda: piece_copy(t).start()))

    def finish():
        at = pl.ds(pl.multiple_of(me * SUBLANES, SUBLANES), SUBLANES)
        pieces[me] = gram[at]
        others(lambda t: remote(gram.at[at], pieces.at[t], rs_send.at[t], rs_recv.at[t], device(t)).wait_recv())
        out_ref[at] = jnp.sum(pieces[...], axis=0) * scale
        others(lambda t: row_copy(t).start())

    owned(me, finish)

    def row_arrived(t):
        at = pl.ds(pl.multiple_of(t * SUBLANES, SUBLANES), SUBLANES)
        remote(out_ref.at[at], out_ref.at[at], ag_send.at[t], ag_recv.at[t], device(t)).wait_recv()

    others(lambda t: owned(t, lambda: row_arrived(t)))

    fy_copy.wait_send()
    for half in halves:
        half.wait_send()

    def sent(j):
        fx_copy(j).wait_send()
        block_copy(j).wait_send()

    loop(1, n_gx, lambda s: sent(lax.rem(gx + s, n_gx)))
    others(lambda t: owned(t, lambda: piece_copy(t).wait_send()))
    owned(me, lambda: others(lambda t: row_copy(t).wait_send()))


def solution(mesh):
    n_gx = mesh.shape["gx"]
    assert mesh.shape["gy"] == CORES

    def local(snapshot, factor_x, factor_y, factor_var):
        local_x, local_y, n_var, depth = snapshot.shape
        n_q = factor_var.shape[1]
        half_p = factor_y.shape[1]
        rank = factor_x.shape[1]
        k = half_p * n_q // n_gx
        total = n_gx * CORES
        scale = 1.0 / (rank * half_p * CORES * n_q)
        f32 = jnp.float32
        block = (n_gx, local_x, k, depth)
        dma = pltpu.SemaphoreType.DMA
        return pl.pallas_call(
            functools.partial(kernel, n_gx, scale),
            out_shape=jax.ShapeDtypeStruct((depth, depth), f32),
            in_specs=[
                pl.BlockSpec(memory_space=pl.ANY),
                pl.BlockSpec(memory_space=pltpu.VMEM),
                pl.BlockSpec(memory_space=pltpu.VMEM),
                pl.BlockSpec(memory_space=pltpu.SMEM),
            ],
            out_specs=pl.BlockSpec(memory_space=pltpu.VMEM),
            scratch_shapes=[
                pltpu.VMEM((local_x, n_var, local_y, depth), f32),
                pltpu.VMEM((n_q, local_y, local_x * depth), f32),
                pltpu.VMEM((n_gx, local_x, 1, depth), f32),
                pltpu.VMEM((half_p, local_y), f32),
                pltpu.VMEM((half_p, local_y), f32),
                pltpu.VMEM(block, f32),
                pltpu.VMEM(block, f32),
                pltpu.VMEM(block, f32),
                pltpu.VMEM(block, f32),
                pltpu.VMEM((depth, depth), f32),
                pltpu.VMEM((total, SUBLANES, depth), f32),
                dma((local_x,)), dma((2,)),
                dma((n_gx,)), dma((n_gx,)),
                dma((n_q,)), dma((n_q,)),
                dma((n_gx,)), dma((n_gx,)),
                dma((total,)), dma((total,)),
                dma((total,)), dma((total,)),
            ],
            compiler_params=pltpu.CompilerParams(
                collective_id=0, has_side_effects=True, vmem_limit_bytes=24 * 1024 * 1024
            ),
        )(jnp.transpose(snapshot, (0, 2, 1, 3)), factor_x, factor_y.T, factor_var)

    in_specs = (P(("snap", "gx"), "gy", None, None), P("gx", None), P(None, "gy"), P())
    return jax.shard_map(local, mesh=mesh, in_specs=in_specs, out_specs=P("snap", None), check_vma=False)
```

```python
import functools

import jax
import jax.numpy as jnp
from jax import lax
from jax.experimental import pallas as pl
from jax.experimental.pallas import tpu as pltpu
from jax.sharding import PartitionSpec as P

MESH = pl.DeviceIdType.MESH
HIGHEST = lax.Precision.HIGHEST
CORES = 2
CHUNKS = 4


def dot(a, b, dims=((1,), (0,))):
    return lax.dot_general(a, b, (dims, ((), ())), precision=HIGHEST, preferred_element_type=jnp.float32)


def loop(first, last, body):
    def step(i, carry):
        body(i)
        return carry

    lax.fori_loop(first, last, step, 0, unroll=(last - first) <= 16)


def kernel(
    n_gx, scale,
    snap_in, fx_in, fyt_in, fv_in, out_ref,
    fx_ref, fyt_ref, fv_ref, snap, reduced, fx_all, fy_send, fy_recv, half_send, half_recv, part, blocks, gram, gram_recv, pieces,
    in_sems, snap_sem, fy_sems, fx_send, fx_recv, half_ssem, half_rsem, a2a_send, a2a_recv, rs_send, rs_recv, core_sems,
):
    gx, gy = lax.axis_index("gx"), lax.axis_index("gy")
    other = 1 - gy
    local_x, n_var, local_y, depth = snap.shape
    n_q = reduced.shape[0]
    _, _, k, _ = blocks.shape
    per_q = n_gx // n_q
    half_rows = depth // CORES

    def remote(src, dst, send, recv, where):
        return pltpu.make_async_remote_copy(
            src_ref=src, dst_ref=dst, send_sem=send, recv_sem=recv, device_id=where, device_id_type=MESH
        )

    small = [
        pltpu.make_async_copy(src, dst, in_sems.at[i])
        for i, (src, dst) in enumerate(((fyt_in, fyt_ref), (fx_in, fx_ref), (fv_in, fv_ref)))
    ]
    for load in small:
        load.start()
    chunk = local_y // CHUNKS
    loads = []
    for x in range(local_x):
        for i in range(CHUNKS):
            at = pl.ds(i * chunk, chunk)
            loads.append(pltpu.make_async_copy(snap_in.at[x, :, at], snap.at[x, :, at], snap_sem.at[x * CHUNKS + i]))
    for load in loads:
        load.start()

    barrier = pltpu.get_barrier_semaphore()
    pl.semaphore_signal(barrier, inc=1, device_id={"gy": other}, device_id_type=MESH)
    loop(1, n_gx, lambda s: pl.semaphore_signal(
        barrier, inc=1, device_id={"gx": lax.rem(gx + s, n_gx)}, device_id_type=MESH))

    for load in small:
        load.wait()
    fx = fx_ref[...]
    rank = fx.shape[1]
    fx_wide = jnp.concatenate([fx, jnp.zeros((local_x, depth - rank), jnp.float32)], axis=1) if rank < depth else fx
    for x in range(local_x):
        fx_all[gx, x] = fx_wide[x : x + 1]
    fy_send[...] = fyt_ref[:, pl.ds(pl.multiple_of(other * local_y, local_y), local_y)]
    fy_mine = fyt_ref[:, pl.ds(pl.multiple_of(gy * local_y, local_y), local_y)]

    pl.semaphore_wait(barrier, n_gx)

    fy_copy = remote(fy_send, fy_recv, fy_sems.at[0], fy_sems.at[1], {"gy": other})
    fy_copy.start()

    def fx_copy(j):
        return remote(fx_all.at[gx], fx_all.at[gx], fx_send.at[j], fx_recv.at[gx], {"gx": j})

    loop(1, n_gx, lambda s: fx_copy(lax.rem(gx + s, n_gx)).start())

    rows = 16
    for part_of, load in enumerate(loads):
        x, first = part_of // CHUNKS, part_of % CHUNKS * chunk
        load.wait()

        def var_step(i, carry, x=x, first=first):
            at = pl.ds(pl.multiple_of(first + i * rows, rows), rows)
            sums = [None] * n_q
            for v in range(n_var):
                cells = snap[x, v, at, :]
                for q in range(n_q):
                    term = cells * fv_ref[q, v]
                    sums[q] = term if v == 0 else sums[q] + term
            for q in range(n_q):
                reduced[q, at, x * depth : (x + 1) * depth] = sums[q]
            return carry

        lax.fori_loop(0, chunk // rows, var_step, 0)

    def put(ref, q, value):
        for x in range(local_x):
            cells = value[:, x * depth : (x + 1) * depth]
            ref[q * per_q : (q + 1) * per_q, x] = cells.reshape(per_q, k, depth)

    fy_copy.wait_recv()
    fy_theirs = fy_recv[...]
    halves = []
    for q in range(n_q):
        put(half_send, q, dot(fy_theirs, reduced[q]))
        at = pl.ds(q * per_q, per_q)
        exchange = remote(half_send.at[at], half_recv.at[at], half_ssem.at[q], half_rsem.at[q], {"gy": other})
        exchange.start()
        halves.append(exchange)
    for q in range(n_q):
        put(part, q, dot(fy_mine, reduced[q]))

    def block_copy(j):
        return remote(part.at[j], blocks.at[gx], a2a_send.at[j], a2a_recv.at[gx], {"gx": j})

    for q in range(n_q):
        at = pl.ds(q * per_q, per_q)
        halves[q].wait_recv()
        part[at] = part[at] + half_recv[at]

        def send_block(j):
            @pl.when(j != gx)
            def _():
                block_copy(j).start()

        loop(q * per_q, (q + 1) * per_q, send_block)
    blocks[gx] = part[gx]

    def arrived(sems, ref, j):
        remote(ref.at[gx], ref.at[j], fx_send.at[j], sems.at[j], {"gx": j}).wait_recv()

    loop(1, n_gx, lambda s: arrived(fx_recv, fx_all, lax.rem(gx + s, n_gx)))
    wide = n_gx * local_x * k
    factor = jnp.broadcast_to(fx_all[...], (n_gx, local_x, k, depth)).reshape(wide, depth)
    largest = jnp.max(jnp.abs(factor), axis=1, keepdims=True)
    largest = jnp.where(largest > 0.0, largest, 1.0)
    unit = factor / largest
    same = (
        lax.broadcasted_iota(jnp.int32, (wide, wide), 0) % k
        == lax.broadcasted_iota(jnp.int32, (wide, wide), 1) % k
    )
    mixing = jnp.where(same, dot(unit, unit, ((1,), (1,))), 0.0)

    loop(1, n_gx, lambda s: arrived(a2a_recv, blocks, lax.rem(gx + s, n_gx)))
    cells = blocks[...].reshape(wide, depth) * largest
    gram[...] = dot(cells, dot(mixing, cells), ((0,), (0,)))

    def others(body):
        loop(1, n_gx, lambda s: body(lax.rem(gx + s, n_gx)))

    my_rows = pl.ds(pl.multiple_of(gy * half_rows, half_rows), half_rows)
    other_rows = pl.ds(pl.multiple_of(other * half_rows, half_rows), half_rows)
    gram_copy = remote(gram.at[other_rows], gram_recv, core_sems.at[0], core_sems.at[1], {"gy": other})
    gram_copy.start()
    gram_copy.wait_recv()
    pieces[gx] = gram[my_rows] + gram_recv[...]

    def piece_copy(t):
        return remote(pieces.at[gx], pieces.at[gx], rs_send.at[t], rs_recv.at[gx], {"gx": t})

    others(lambda t: piece_copy(t).start())
    others(lambda t: remote(pieces.at[gx], pieces.at[t], rs_send.at[t], rs_recv.at[t], {"gx": t}).wait_recv())
    out_ref[my_rows] = jnp.sum(pieces[...], axis=0) * scale
    out_copy = remote(out_ref.at[my_rows], out_ref.at[my_rows], core_sems.at[2], core_sems.at[3], {"gy": other})
    out_copy.start()

    fy_copy.wait_send()
    for exchange in halves:
        exchange.wait_send()

    def sent(j):
        fx_copy(j).wait_send()
        block_copy(j).wait_send()

    loop(1, n_gx, lambda s: sent(lax.rem(gx + s, n_gx)))
    others(lambda t: piece_copy(t).wait_send())
    gram_copy.wait_send()
    out_copy.wait_send()
    remote(out_ref.at[my_rows], out_ref.at[other_rows], core_sems.at[2], core_sems.at[3], {"gy": other}).wait_recv()


def solution(mesh):
    n_gx = mesh.shape["gx"]
    assert mesh.shape["gy"] == CORES

    def local(snapshot, factor_x, factor_y, factor_var):
        local_x, local_y, n_var, depth = snapshot.shape
        n_q = factor_var.shape[1]
        half_p = factor_y.shape[1]
        rank = factor_x.shape[1]
        k = half_p * n_q // n_gx
        scale = 1.0 / (rank * half_p * CORES * n_q)
        f32 = jnp.float32
        block = (n_gx, local_x, k, depth)
        dma = pltpu.SemaphoreType.DMA
        return pl.pallas_call(
            functools.partial(kernel, n_gx, scale),
            out_shape=jax.ShapeDtypeStruct((depth, depth), f32),
            in_specs=[
                pl.BlockSpec(memory_space=pltpu.HBM),
                pl.BlockSpec(memory_space=pltpu.HBM),
                pl.BlockSpec(memory_space=pltpu.HBM),
                pl.BlockSpec(memory_space=pltpu.HBM),
            ],
            out_specs=pl.BlockSpec(memory_space=pltpu.VMEM),
            scratch_shapes=[
                pltpu.VMEM(factor_x.shape, f32),
                pltpu.VMEM((half_p, local_y * CORES), f32),
                pltpu.SMEM((n_q, n_var), f32),
                pltpu.VMEM((local_x, n_var, local_y, depth), f32),
                pltpu.VMEM((n_q, local_y, local_x * depth), f32),
                pltpu.VMEM((n_gx, local_x, 1, depth), f32),
                pltpu.VMEM((half_p, local_y), f32),
                pltpu.VMEM((half_p, local_y), f32),
                pltpu.VMEM(block, f32),
                pltpu.VMEM(block, f32),
                pltpu.VMEM(block, f32),
                pltpu.VMEM(block, f32),
                pltpu.VMEM((depth, depth), f32),
                pltpu.VMEM((depth // CORES, depth), f32),
                pltpu.VMEM((n_gx, depth // CORES, depth), f32),
                dma((3,)), dma((local_x * CHUNKS,)), dma((2,)),
                dma((n_gx,)), dma((n_gx,)),
                dma((n_q,)), dma((n_q,)),
                dma((n_gx,)), dma((n_gx,)),
                dma((n_gx,)), dma((n_gx,)),
                dma((4,)),
            ],
            compiler_params=pltpu.CompilerParams(
                collective_id=0, has_side_effects=True, vmem_limit_bytes=24 * 1024 * 1024
            ),
        )(*[pltpu.with_memory_space_constraint(a, pltpu.HBM) for a in (jnp.transpose(snapshot, (0, 2, 1, 3)), factor_x, factor_y.T, factor_var.T)])

    in_specs = (P(("snap", "gx"), "gy", None, None), P("gx", None), P(None, "gy"), P())
    return jax.shard_map(local, mesh=mesh, in_specs=in_specs, out_specs=P("snap", None), check_vma=False)
```

```python
import functools

import jax
import jax.numpy as jnp
from jax import lax
from jax.experimental import pallas as pl
from jax.experimental.pallas import tpu as pltpu
from jax.sharding import PartitionSpec as P

MESH = pl.DeviceIdType.MESH
HIGHEST = lax.Precision.HIGHEST
CORES = 2
CHUNKS = 4


def dot(a, b, dims=((1,), (0,))):
    return lax.dot_general(a, b, (dims, ((), ())), precision=HIGHEST, preferred_element_type=jnp.float32)


def dot3(a, b, dims=((1,), (0,))):
    def part(x, y):
        return lax.dot_general(x, y, (dims, ((), ())), preferred_element_type=jnp.float32)

    a_high, b_high = a.astype(jnp.bfloat16), b.astype(jnp.bfloat16)
    a_low = (a - a_high.astype(jnp.float32)).astype(jnp.bfloat16)
    b_low = (b - b_high.astype(jnp.float32)).astype(jnp.bfloat16)
    return part(a_high, b_high) + (part(a_high, b_low) + part(a_low, b_high))


def flip(i, s, n):
    found, digit = 0, 1
    while digit < n:
        found = found + digit * ((i // digit + s // digit) % 2)
        digit *= 2
    return found


def loop(first, last, body):
    def step(i, carry):
        body(i)
        return carry

    lax.fori_loop(first, last, step, 0, unroll=(last - first) <= 16)


def kernel(
    n_gx, scale,
    snap_in, fx_in, fyt_in, fv_in, out_ref,
    fx_ref, fyt_ref, fv_ref, snap, reduced, fx_all, fy_recv, half_send, half_recv, part, blocks, gram, gram_recv, pieces, summed,
    in_sems, snap_sem, fy_sems, fx_send, fx_recv, half_ssem, half_rsem, a2a_send, a2a_recv, rs_send, rs_recv, core_sems,
):
    gx, gy = lax.axis_index("gx"), lax.axis_index("gy")
    other = 1 - gy
    local_x, n_var, local_y, depth = snap.shape
    n_q = reduced.shape[0]
    _, _, k, _ = blocks.shape
    per_q = n_gx // n_q
    half_rows = depth * 5 // 8 // CORES

    def remote(src, dst, send, recv, where):
        return pltpu.make_async_remote_copy(
            src_ref=src, dst_ref=dst, send_sem=send, recv_sem=recv, device_id=where, device_id_type=MESH
        )

    small = [
        pltpu.make_async_copy(src, dst, in_sems.at[i])
        for i, (src, dst) in enumerate(((fyt_in, fyt_ref), (fx_in, fx_ref), (fv_in, fv_ref)))
    ]
    for load in small:
        load.start()
    chunk = local_y // CHUNKS
    loads = []
    for x in range(local_x):
        for i in range(CHUNKS):
            at = pl.ds(i * chunk, chunk)
            loads.append(pltpu.make_async_copy(snap_in.at[x, :, at], snap.at[x, :, at], snap_sem.at[x * CHUNKS + i]))
    for load in loads:
        load.start()

    barrier = pltpu.get_barrier_semaphore()
    pl.semaphore_signal(barrier, inc=1, device_id={"gy": other}, device_id_type=MESH)
    loop(1, n_gx, lambda s: pl.semaphore_signal(
        barrier, inc=1, device_id={"gx": lax.rem(gx + s, n_gx)}, device_id_type=MESH))

    pl.semaphore_wait(barrier, n_gx)
    other_y = pl.ds(pl.multiple_of(other * local_y, local_y), local_y)
    fy_copy = remote(fyt_in.at[:, other_y], fy_recv, fy_sems.at[0], fy_sems.at[1], {"gy": other})
    fy_copy.start()
    for load in small:
        load.wait()
    fx = fx_ref[...]
    rank = fx.shape[1]
    fx_wide = jnp.concatenate([fx, jnp.zeros((local_x, depth - rank), jnp.float32)], axis=1) if rank < depth else fx
    for x in range(local_x):
        fx_all[gx, x] = fx_wide[x : x + 1]
    fy_mine = fyt_ref[:, pl.ds(pl.multiple_of(gy * local_y, local_y), local_y)]

    def fx_copy(j):
        return remote(fx_all.at[gx], fx_all.at[gx], fx_send.at[j], fx_recv.at[gx], {"gx": j})

    loop(1, n_gx, lambda s: fx_copy(lax.rem(gx + s, n_gx)).start())

    rows = 16
    for part_of, load in enumerate(loads):
        x, first = part_of // CHUNKS, part_of % CHUNKS * chunk
        load.wait()

        def var_step(i, carry, x=x, first=first):
            at = pl.ds(pl.multiple_of(first + i * rows, rows), rows)
            sums = [None] * n_q
            for v in range(n_var):
                cells = snap[x, v, at, :]
                for q in range(n_q):
                    term = cells * fv_ref[q, v]
                    sums[q] = term if v == 0 else sums[q] + term
            for q in range(n_q):
                reduced[q, at, x * depth : (x + 1) * depth] = sums[q]
            return carry

        lax.fori_loop(0, chunk // rows, var_step, 0)

    def put(ref, q, value):
        for x in range(local_x):
            cells = value[:, x * depth : (x + 1) * depth]
            ref[pl.ds(q * per_q, per_q), x] = cells.reshape(per_q, k, depth)

    fy_copy.wait_recv()
    fy_theirs = fy_recv[...]
    halves = []
    order = range(n_q)
    for q in order:
        put(half_send, q, dot3(fy_theirs, reduced[q]))
        at = pl.ds(q * per_q, per_q)
        exchange = remote(half_send.at[at], half_recv.at[at], half_ssem.at[q], half_rsem.at[q], {"gy": other})
        exchange.start()
        halves.append(exchange)
    for q in order:
        put(part, q, dot3(fy_mine, reduced[q]))

    def block_copy(j):
        return remote(part.at[j], blocks.at[gx], a2a_send.at[j], a2a_recv.at[gx], {"gx": j})

    for q, exchange in zip(order, halves):
        at = pl.ds(q * per_q, per_q)
        exchange.wait_recv()
        part[at] = part[at] + half_recv[at]

        def send_block(j):
            @pl.when(j != gx)
            def _():
                block_copy(j).start()

        loop(0, per_q, lambda i, q=q: send_block(q * per_q + i))
    blocks[gx] = part[gx]

    def arrived(sems, ref, j):
        remote(ref.at[gx], ref.at[j], fx_send.at[j], sems.at[j], {"gx": j}).wait_recv()

    loop(1, n_gx, lambda s: arrived(fx_recv, fx_all, lax.rem(gx + s, n_gx)))
    wide = n_gx * local_x * k
    factor = jnp.broadcast_to(fx_all[...], (n_gx, local_x, k, depth)).reshape(wide, depth)
    largest = jnp.max(jnp.abs(factor), axis=1, keepdims=True)
    largest = jnp.where(largest > 0.0, largest, 1.0)
    unit = factor / largest
    same = (
        lax.broadcasted_iota(jnp.int32, (wide, wide), 0) % k
        == lax.broadcasted_iota(jnp.int32, (wide, wide), 1) % k
    )
    mixing = jnp.where(same, dot(unit, unit, ((1,), (1,))), 0.0)

    loop(1, n_gx, lambda s: arrived(a2a_recv, blocks, lax.rem(gx + s, n_gx)))
    cells = blocks[...].reshape(wide, depth) * largest
    square = dot3(cells, dot3(mixing, cells), ((0,), (0,)))
    side = depth // 4
    lane = lax.broadcasted_iota(jnp.int32, (side, depth), 1)
    gram[:side] = square[:side]
    gram[side : 2 * side] = jnp.where(lane < side, pltpu.roll(square[3 * side :], side, 1), square[side : 2 * side])
    third, split = square[2 * side : 3 * side], side // 2
    gram[2 * side :] = jnp.where(lane[:split] < 2 * side, pltpu.roll(third[split:], 2 * side, 1), third[:split])

    def others(body):
        loop(1, n_gx, lambda s: body(flip(gx, s, n_gx)))

    my_rows = pl.ds(pl.multiple_of(gy * half_rows, half_rows), half_rows)
    other_rows = pl.ds(pl.multiple_of(other * half_rows, half_rows), half_rows)
    gram_copy = remote(gram.at[other_rows], gram_recv, core_sems.at[0], core_sems.at[1], {"gy": other})
    gram_copy.start()
    gram_copy.wait_recv()
    pieces[gx] = gram[my_rows] + gram_recv[...]

    def piece_copy(t):
        return remote(pieces.at[gx], pieces.at[gx], rs_send.at[t], rs_recv.at[gx], {"gx": t})

    others(lambda t: piece_copy(t).start())
    others(lambda t: remote(pieces.at[gx], pieces.at[t], rs_send.at[t], rs_recv.at[t], {"gx": t}).wait_recv())
    summed[my_rows] = jnp.sum(pieces[...], axis=0) * scale
    out_copy = remote(summed.at[my_rows], summed.at[my_rows], core_sems.at[2], core_sems.at[3], {"gy": other})
    out_copy.start()

    fy_copy.wait_send()
    for exchange in halves:
        exchange.wait_send()

    def sent(j):
        fx_copy(j).wait_send()
        block_copy(j).wait_send()

    loop(1, n_gx, lambda s: sent(lax.rem(gx + s, n_gx)))
    others(lambda t: piece_copy(t).wait_send())
    gram_copy.wait_send()
    remote(summed.at[my_rows], summed.at[other_rows], core_sems.at[2], core_sems.at[3], {"gy": other}).wait_recv()
    third = summed[2 * side :]
    upper = jnp.concatenate([
        summed[: 2 * side], third, pltpu.roll(third, 2 * side, 1), pltpu.roll(summed[side : 2 * side], depth - side, 1)
    ], axis=0)
    row_block = lax.broadcasted_iota(jnp.int32, (depth, depth), 0) // side
    lane_block = lax.broadcasted_iota(jnp.int32, (depth, depth), 1) // side
    out_ref[...] = jnp.where(row_block > lane_block, upper.T, upper)
    out_copy.wait_send()


def solution(mesh):
    n_gx = mesh.shape["gx"]
    assert mesh.shape["gy"] == CORES

    def local(snapshot, factor_x, factor_y, factor_var):
        local_x, local_y, n_var, depth = snapshot.shape
        n_q = factor_var.shape[1]
        half_p = factor_y.shape[1]
        rank = factor_x.shape[1]
        k = half_p * n_q // n_gx
        scale = 1.0 / (rank * half_p * CORES * n_q)
        f32 = jnp.float32
        block = (n_gx, local_x, k, depth)
        packed = depth * 5 // 8
        dma = pltpu.SemaphoreType.DMA
        return pl.pallas_call(
            functools.partial(kernel, n_gx, scale),
            out_shape=jax.ShapeDtypeStruct((depth, depth), f32),
            in_specs=[
                pl.BlockSpec(memory_space=pltpu.HBM),
                pl.BlockSpec(memory_space=pltpu.HBM),
                pl.BlockSpec(memory_space=pltpu.HBM),
                pl.BlockSpec(memory_space=pltpu.HBM),
            ],
            out_specs=pl.BlockSpec(memory_space=pltpu.VMEM),
            scratch_shapes=[
                pltpu.VMEM(factor_x.shape, f32),
                pltpu.VMEM((half_p, local_y * CORES), f32),
                pltpu.SMEM((n_q, n_var), f32),
                pltpu.VMEM((local_x, n_var, local_y, depth), f32),
                pltpu.VMEM((n_q, local_y, local_x * depth), f32),
                pltpu.VMEM((n_gx, local_x, 1, depth), f32),
                pltpu.VMEM((half_p, local_y), f32),
                pltpu.VMEM(block, f32),
                pltpu.VMEM(block, f32),
                pltpu.VMEM(block, f32),
                pltpu.VMEM(block, f32),
                pltpu.VMEM((packed, depth), f32),
                pltpu.VMEM((packed // CORES, depth), f32),
                pltpu.VMEM((n_gx, packed // CORES, depth), f32),
                pltpu.VMEM((packed, depth), f32),
                dma((3,)), dma((local_x * CHUNKS,)), dma((2,)),
                dma((n_gx,)), dma((n_gx,)),
                dma((n_q,)), dma((n_q,)),
                dma((n_gx,)), dma((n_gx,)),
                dma((n_gx,)), dma((n_gx,)),
                dma((4,)),
            ],
            compiler_params=pltpu.CompilerParams(
                collective_id=0, has_side_effects=True, vmem_limit_bytes=24 * 1024 * 1024
            ),
        )(*[pltpu.with_memory_space_constraint(a, pltpu.HBM) for a in (jnp.transpose(snapshot, (0, 2, 1, 3)), factor_x, factor_y.T, factor_var.T)])

    in_specs = (P(("snap", "gx"), "gy", None, None), P("gx", None), P(None, "gy"), P())
    return jax.shard_map(local, mesh=mesh, in_specs=in_specs, out_specs=P("snap", None), check_vma=False)
```

```python
import functools

import jax
import jax.numpy as jnp
from jax import lax
from jax.experimental import pallas as pl
from jax.experimental.pallas import tpu as pltpu
from jax.sharding import PartitionSpec as P

MESH = pl.DeviceIdType.MESH
HIGHEST = lax.Precision.HIGHEST
CORES = 2
CHUNKS = 4


def dot(a, b, dims=((1,), (0,))):
    return lax.dot_general(a, b, (dims, ((), ())), precision=HIGHEST, preferred_element_type=jnp.float32)


def dot3(a, b, dims=((1,), (0,))):
    def part(x, y):
        return lax.dot_general(x, y, (dims, ((), ())), preferred_element_type=jnp.float32)

    a_high, b_high = a.astype(jnp.bfloat16), b.astype(jnp.bfloat16)
    a_low = (a - a_high.astype(jnp.float32)).astype(jnp.bfloat16)
    b_low = (b - b_high.astype(jnp.float32)).astype(jnp.bfloat16)
    return part(a_high, b_high) + (part(a_high, b_low) + part(a_low, b_high))


def loop(first, last, body):
    def step(i, carry):
        body(i)
        return carry

    lax.fori_loop(first, last, step, 0, unroll=(last - first) <= 16)


def kernel(
    n_gx, scale,
    snap_in, fx_in, fyt_in, fv_in, out_ref,
    fx_ref, fyt_ref, fv_ref, snap, reduced, fx_all, fy_recv, half_send, half_recv, part, blocks, gram, gram_recv, pieces, summed,
    in_sems, snap_sem, fy_sems, fx_send, fx_recv, half_ssem, half_rsem, a2a_send, a2a_recv, rs_send, rs_recv, core_sems,
):
    gx, gy = lax.axis_index("gx"), lax.axis_index("gy")
    other = 1 - gy
    local_x, n_var, local_y, depth = snap.shape
    n_q = reduced.shape[0]
    _, _, k, _ = blocks.shape
    per_q = n_gx // n_q
    half_rows = depth * 5 // 8 // CORES

    def remote(src, dst, send, recv, where):
        return pltpu.make_async_remote_copy(
            src_ref=src, dst_ref=dst, send_sem=send, recv_sem=recv, device_id=where, device_id_type=MESH
        )

    small = [
        pltpu.make_async_copy(src, dst, in_sems.at[i])
        for i, (src, dst) in enumerate(((fyt_in, fyt_ref), (fx_in, fx_ref), (fv_in, fv_ref)))
    ]
    for load in small:
        load.start()
    chunk = local_y // CHUNKS
    loads = []
    for x in range(local_x):
        for i in range(CHUNKS):
            at = pl.ds(i * chunk, chunk)
            loads.append(pltpu.make_async_copy(snap_in.at[x, :, at], snap.at[x, :, at], snap_sem.at[x * CHUNKS + i]))
    for load in loads:
        load.start()

    barrier = pltpu.get_barrier_semaphore()
    pl.semaphore_signal(barrier, inc=1, device_id={"gy": other}, device_id_type=MESH)
    loop(1, n_gx, lambda s: pl.semaphore_signal(
        barrier, inc=1, device_id={"gx": lax.rem(gx + s, n_gx)}, device_id_type=MESH))

    pl.semaphore_wait(barrier, n_gx)
    other_y = pl.ds(pl.multiple_of(other * local_y, local_y), local_y)
    fy_copy = remote(fyt_in.at[:, other_y], fy_recv, fy_sems.at[0], fy_sems.at[1], {"gy": other})
    fy_copy.start()
    for load in small:
        load.wait()
    fx = fx_ref[...]
    rank = fx.shape[1]
    fx_wide = jnp.concatenate([fx, jnp.zeros((local_x, depth - rank), jnp.float32)], axis=1) if rank < depth else fx
    for x in range(local_x):
        fx_all[gx, x] = fx_wide[x : x + 1]
    fy_mine = fyt_ref[:, pl.ds(pl.multiple_of(gy * local_y, local_y), local_y)]

    def fx_copy(j):
        return remote(fx_all.at[gx], fx_all.at[gx], fx_send.at[j], fx_recv.at[gx], {"gx": j})

    loop(1, n_gx, lambda s: fx_copy(lax.rem(gx + s, n_gx)).start())

    rows = 16
    for part_of, load in enumerate(loads):
        x, first = part_of // CHUNKS, part_of % CHUNKS * chunk
        load.wait()

        def var_step(i, carry, x=x, first=first):
            at = pl.ds(pl.multiple_of(first + i * rows, rows), rows)
            sums = [None] * n_q
            for v in range(n_var):
                cells = snap[x, v, at, :]
                for q in range(n_q):
                    term = cells * fv_ref[q, v]
                    sums[q] = term if v == 0 else sums[q] + term
            for q in range(n_q):
                reduced[q, at, x * depth : (x + 1) * depth] = sums[q]
            return carry

        lax.fori_loop(0, chunk // rows, var_step, 0)

    def put(ref, q, value):
        for x in range(local_x):
            cells = value[:, x * depth : (x + 1) * depth]
            ref[pl.ds(q * per_q, per_q), x] = cells.reshape(per_q, k, depth)

    fy_copy.wait_recv()
    fy_theirs = fy_recv[...]
    halves = []
    for q in range(n_q):
        put(half_send, q, dot3(fy_theirs, reduced[q]))
        at = pl.ds(q * per_q, per_q)
        exchange = remote(half_send.at[at], half_recv.at[at], half_ssem.at[q], half_rsem.at[q], {"gy": other})
        exchange.start()
        halves.append(exchange)
    for q in range(n_q):
        put(part, q, dot3(fy_mine, reduced[q]))

    def block_copy(j):
        return remote(part.at[j], blocks.at[gx], a2a_send.at[j], a2a_recv.at[gx], {"gx": j})

    for q, exchange in enumerate(halves):
        at = pl.ds(q * per_q, per_q)
        exchange.wait_recv()
        part[at] = part[at] + half_recv[at]

        def send_block(j):
            @pl.when(j != gx)
            def _():
                block_copy(j).start()

        loop(0, per_q, lambda i, q=q: send_block(q * per_q + i))
    blocks[gx] = part[gx]

    def arrived(sems, ref, j):
        remote(ref.at[gx], ref.at[j], fx_send.at[j], sems.at[j], {"gx": j}).wait_recv()

    loop(1, n_gx, lambda s: arrived(fx_recv, fx_all, lax.rem(gx + s, n_gx)))
    wide = n_gx * local_x * k
    factor = jnp.broadcast_to(fx_all[...], (n_gx, local_x, k, depth)).reshape(wide, depth)
    largest = jnp.max(jnp.abs(factor), axis=1, keepdims=True)
    largest = jnp.where(largest > 0.0, largest, 1.0)
    unit = factor / largest
    same = (
        lax.broadcasted_iota(jnp.int32, (wide, wide), 0) % k
        == lax.broadcasted_iota(jnp.int32, (wide, wide), 1) % k
    )
    mixing = jnp.where(same, dot(unit, unit, ((1,), (1,))), 0.0)

    loop(1, n_gx, lambda s: arrived(a2a_recv, blocks, lax.rem(gx + s, n_gx)))
    cells = blocks[...].reshape(wide, depth) * largest
    square = dot3(cells, dot3(mixing, cells), ((0,), (0,)))
    side = depth // 4
    lane = lax.broadcasted_iota(jnp.int32, (side, depth), 1)
    gram[:side] = square[:side]
    gram[side : 2 * side] = jnp.where(lane < side, pltpu.roll(square[3 * side :], side, 1), square[side : 2 * side])
    third, split = square[2 * side : 3 * side], side // 2
    gram[2 * side :] = jnp.where(lane[:split] < 2 * side, pltpu.roll(third[split:], 2 * side, 1), third[:split])

    def others(body):
        loop(1, n_gx, lambda s: body(lax.rem(gx + s, n_gx)))

    my_rows = pl.ds(pl.multiple_of(gy * half_rows, half_rows), half_rows)
    other_rows = pl.ds(pl.multiple_of(other * half_rows, half_rows), half_rows)
    gram_copy = remote(gram.at[other_rows], gram_recv, core_sems.at[0], core_sems.at[1], {"gy": other})
    gram_copy.start()
    gram_copy.wait_recv()
    pieces[gx] = gram[my_rows] + gram_recv[...]

    def piece_copy(t):
        return remote(pieces.at[gx], pieces.at[gx], rs_send.at[t], rs_recv.at[gx], {"gx": t})

    others(lambda t: piece_copy(t).start())
    others(lambda t: remote(pieces.at[gx], pieces.at[t], rs_send.at[t], rs_recv.at[t], {"gx": t}).wait_recv())
    summed[my_rows] = jnp.sum(pieces[...], axis=0) * scale
    out_copy = remote(summed.at[my_rows], summed.at[my_rows], core_sems.at[2], core_sems.at[3], {"gy": other})
    out_copy.start()

    fy_copy.wait_send()
    for exchange in halves:
        exchange.wait_send()

    def sent(j):
        fx_copy(j).wait_send()
        block_copy(j).wait_send()

    loop(1, n_gx, lambda s: sent(lax.rem(gx + s, n_gx)))
    others(lambda t: piece_copy(t).wait_send())
    gram_copy.wait_send()
    remote(summed.at[my_rows], summed.at[other_rows], core_sems.at[2], core_sems.at[3], {"gy": other}).wait_recv()
    third = summed[2 * side :]
    upper = jnp.concatenate([
        summed[: 2 * side], third, pltpu.roll(third, 2 * side, 1), pltpu.roll(summed[side : 2 * side], depth - side, 1)
    ], axis=0)
    row_block = lax.broadcasted_iota(jnp.int32, (depth, depth), 0) // side
    lane_block = lax.broadcasted_iota(jnp.int32, (depth, depth), 1) // side
    out_ref[...] = jnp.where(row_block > lane_block, upper.T, upper)
    out_copy.wait_send()


def solution(mesh):
    n_gx = mesh.shape["gx"]
    assert mesh.shape["gy"] == CORES

    def local(snapshot, factor_x, factor_y, factor_var):
        local_x, local_y, n_var, depth = snapshot.shape
        n_q = factor_var.shape[1]
        half_p = factor_y.shape[1]
        rank = factor_x.shape[1]
        k = half_p * n_q // n_gx
        scale = 1.0 / (rank * half_p * CORES * n_q)
        f32 = jnp.float32
        block = (n_gx, local_x, k, depth)
        packed = depth * 5 // 8
        dma = pltpu.SemaphoreType.DMA
        return pl.pallas_call(
            functools.partial(kernel, n_gx, scale),
            out_shape=jax.ShapeDtypeStruct((depth, depth), f32),
            in_specs=[
                pl.BlockSpec(memory_space=pltpu.HBM),
                pl.BlockSpec(memory_space=pltpu.HBM),
                pl.BlockSpec(memory_space=pltpu.HBM),
                pl.BlockSpec(memory_space=pltpu.HBM),
            ],
            out_specs=pl.BlockSpec(memory_space=pltpu.VMEM),
            scratch_shapes=[
                pltpu.VMEM(factor_x.shape, f32),
                pltpu.VMEM((half_p, local_y * CORES), f32),
                pltpu.SMEM((n_q, n_var), f32),
                pltpu.VMEM((local_x, n_var, local_y, depth), f32),
                pltpu.VMEM((n_q, local_y, local_x * depth), f32),
                pltpu.VMEM((n_gx, local_x, 1, depth), f32),
                pltpu.VMEM((half_p, local_y), f32),
                pltpu.VMEM(block, f32),
                pltpu.VMEM(block, f32),
                pltpu.VMEM(block, f32),
                pltpu.VMEM(block, f32),
                pltpu.VMEM((packed, depth), f32),
                pltpu.VMEM((packed // CORES, depth), f32),
                pltpu.VMEM((n_gx, packed // CORES, depth), f32),
                pltpu.VMEM((packed, depth), f32),
                dma((3,)), dma((local_x * CHUNKS,)), dma((2,)),
                dma((n_gx,)), dma((n_gx,)),
                dma((n_q,)), dma((n_q,)),
                dma((n_gx,)), dma((n_gx,)),
                dma((n_gx,)), dma((n_gx,)),
                dma((4,)),
            ],
            compiler_params=pltpu.CompilerParams(
                collective_id=0, has_side_effects=True, vmem_limit_bytes=24 * 1024 * 1024
            ),
        )(*[pltpu.with_memory_space_constraint(a, pltpu.HBM) for a in (jnp.transpose(snapshot, (0, 2, 1, 3)), factor_x, factor_y.T, factor_var.T)])

    in_specs = (P(("snap", "gx"), "gy", None, None), P("gx", None), P(None, "gy"), P())
    return jax.shard_map(local, mesh=mesh, in_specs=in_specs, out_specs=P("snap", None), check_vma=False)
```

```python
import functools

import jax
import jax.numpy as jnp
from jax import lax
from jax.experimental import pallas as pl
from jax.experimental.pallas import tpu as pltpu
from jax.sharding import PartitionSpec as P

MESH = pl.DeviceIdType.MESH
HIGHEST = lax.Precision.HIGHEST
CORES = 2
CHUNKS = 4


def dot(a, b, dims=((1,), (0,))):
    return lax.dot_general(a, b, (dims, ((), ())), precision=HIGHEST, preferred_element_type=jnp.float32)


def dot3(a, b, dims=((1,), (0,))):
    def part(x, y):
        return lax.dot_general(x, y, (dims, ((), ())), preferred_element_type=jnp.float32)

    a_high, b_high = a.astype(jnp.bfloat16), b.astype(jnp.bfloat16)
    a_low = (a - a_high.astype(jnp.float32)).astype(jnp.bfloat16)
    b_low = (b - b_high.astype(jnp.float32)).astype(jnp.bfloat16)
    return part(a_high, b_high) + (part(a_high, b_low) + part(a_low, b_high))


def loop(first, last, body):
    def step(i, carry):
        body(i)
        return carry

    lax.fori_loop(first, last, step, 0, unroll=(last - first) <= 16)


def kernel(
    n_gx, scale,
    snap_in, fx_in, fyt_in, fv_in, out_ref,
    fx_ref, fyt_ref, fv_ref, snap, reduced, fx_all, fy_recv, half_send, half_recv, part, blocks, gram, gram_recv, pieces, summed,
    in_sems, snap_sem, fy_sems, fx_send, fx_recv, half_ssem, half_rsem, a2a_send, a2a_recv, rs_send, rs_recv, core_sems,
):
    gx, gy = lax.axis_index("gx"), lax.axis_index("gy")
    other = 1 - gy
    local_x, n_var, local_y, depth = snap.shape
    n_q = reduced.shape[0]
    _, _, k, _ = blocks.shape
    per_q = n_gx // n_q
    half_rows = depth * 5 // 8 // CORES

    def remote(src, dst, send, recv, where):
        return pltpu.make_async_remote_copy(
            src_ref=src, dst_ref=dst, send_sem=send, recv_sem=recv, device_id=where, device_id_type=MESH
        )

    small = [
        pltpu.make_async_copy(src, dst, in_sems.at[i])
        for i, (src, dst) in enumerate(((fyt_in, fyt_ref), (fx_in, fx_ref), (fv_in, fv_ref)))
    ]
    for load in small:
        load.start()
    chunk = local_y // CHUNKS
    loads = []
    for x in range(local_x):
        for i in range(CHUNKS):
            at = pl.ds(i * chunk, chunk)
            loads.append(pltpu.make_async_copy(snap_in.at[x, :, at], snap.at[x, :, at], snap_sem.at[x * CHUNKS + i]))
    for load in loads:
        load.start()

    barrier = pltpu.get_barrier_semaphore()
    pl.semaphore_signal(barrier, inc=1, device_id={"gy": other}, device_id_type=MESH)
    loop(1, n_gx, lambda s: pl.semaphore_signal(
        barrier, inc=1, device_id={"gx": lax.rem(gx + s, n_gx)}, device_id_type=MESH))

    pl.semaphore_wait(barrier, n_gx)
    other_y = pl.ds(pl.multiple_of(other * local_y, local_y), local_y)
    fy_copy = remote(fyt_in.at[:, other_y], fy_recv, fy_sems.at[0], fy_sems.at[1], {"gy": other})
    fy_copy.start()
    for load in small:
        load.wait()
    fx = fx_ref[...]
    rank = fx.shape[1]
    fx_wide = jnp.concatenate([fx, jnp.zeros((local_x, depth - rank), jnp.float32)], axis=1) if rank < depth else fx
    for x in range(local_x):
        fx_all[gx, x] = fx_wide[x : x + 1]
    fy_mine = fyt_ref[:, pl.ds(pl.multiple_of(gy * local_y, local_y), local_y)]

    def fx_copy(j):
        return remote(fx_all.at[gx], fx_all.at[gx], fx_send.at[j], fx_recv.at[gx], {"gx": j})

    loop(1, n_gx, lambda s: fx_copy(lax.rem(gx + s, n_gx)).start())

    rows = 32
    for part_of, load in enumerate(loads):
        x, first = part_of // CHUNKS, part_of % CHUNKS * chunk
        load.wait()

        def var_step(i, carry, x=x, first=first):
            at = pl.ds(pl.multiple_of(first + i * rows, rows), rows)
            sums = [None] * n_q
            for v in range(n_var):
                cells = snap[x, v, at, :]
                for q in range(n_q):
                    term = cells * fv_ref[q, v]
                    sums[q] = term if v == 0 else sums[q] + term
            for q in range(n_q):
                reduced[q, at, x * depth : (x + 1) * depth] = sums[q]
            return carry

        lax.fori_loop(0, chunk // rows, var_step, 0)

    def put(ref, q, value):
        for x in range(local_x):
            cells = value[:, x * depth : (x + 1) * depth]
            ref[pl.ds(q * per_q, per_q), x] = cells.reshape(per_q, k, depth)

    fy_copy.wait_recv()
    fy_both = jnp.concatenate([fy_recv[...], fy_mine], axis=0)
    half_p = fy_recv.shape[0]
    halves = []
    for q in range(n_q):
        both = dot(fy_both, reduced[q])
        put(half_send, q, both[:half_p])
        put(part, q, both[half_p:])
        at = pl.ds(q * per_q, per_q)
        exchange = remote(half_send.at[at], half_recv.at[at], half_ssem.at[q], half_rsem.at[q], {"gy": other})
        exchange.start()
        halves.append(exchange)

    def block_copy(j):
        return remote(part.at[j], blocks.at[gx], a2a_send.at[j], a2a_recv.at[gx], {"gx": j})

    for q, exchange in enumerate(halves):
        at = pl.ds(q * per_q, per_q)
        exchange.wait_recv()
        part[at] = part[at] + half_recv[at]

        def send_block(j):
            @pl.when(j != gx)
            def _():
                block_copy(j).start()

        loop(0, per_q, lambda i, q=q: send_block(q * per_q + i))
    blocks[gx] = part[gx]

    def arrived(sems, ref, j):
        remote(ref.at[gx], ref.at[j], fx_send.at[j], sems.at[j], {"gx": j}).wait_recv()

    loop(1, n_gx, lambda s: arrived(fx_recv, fx_all, lax.rem(gx + s, n_gx)))
    wide = n_gx * local_x * k
    factor = jnp.broadcast_to(fx_all[...], (n_gx, local_x, k, depth)).reshape(wide, depth)
    largest = jnp.max(jnp.abs(factor), axis=1, keepdims=True)
    largest = jnp.where(largest > 0.0, largest, 1.0)
    unit = factor / largest
    same = (
        lax.broadcasted_iota(jnp.int32, (wide, wide), 0) % k
        == lax.broadcasted_iota(jnp.int32, (wide, wide), 1) % k
    )
    mixing = jnp.where(same, dot(unit, unit, ((1,), (1,))), 0.0)

    loop(1, n_gx, lambda s: arrived(a2a_recv, blocks, lax.rem(gx + s, n_gx)))
    cells = blocks[...].reshape(wide, depth) * largest
    square = dot3(cells, dot3(mixing, cells), ((0,), (0,)))
    side = depth // 4
    lane = lax.broadcasted_iota(jnp.int32, (side, depth), 1)
    gram[:side] = square[:side]
    gram[side : 2 * side] = jnp.where(lane < side, pltpu.roll(square[3 * side :], side, 1), square[side : 2 * side])
    third, split = square[2 * side : 3 * side], side // 2
    gram[2 * side :] = jnp.where(lane[:split] < 2 * side, pltpu.roll(third[split:], 2 * side, 1), third[:split])

    def others(body):
        loop(1, n_gx, lambda s: body(lax.rem(gx + s, n_gx)))

    my_rows = pl.ds(pl.multiple_of(gy * half_rows, half_rows), half_rows)
    other_rows = pl.ds(pl.multiple_of(other * half_rows, half_rows), half_rows)
    gram_copy = remote(gram.at[other_rows], gram_recv, core_sems.at[0], core_sems.at[1], {"gy": other})
    gram_copy.start()
    gram_copy.wait_recv()
    pieces[gx] = gram[my_rows] + gram_recv[...]

    def piece_copy(t):
        return remote(pieces.at[gx], pieces.at[gx], rs_send.at[t], rs_recv.at[gx], {"gx": t})

    others(lambda t: piece_copy(t).start())
    others(lambda t: remote(pieces.at[gx], pieces.at[t], rs_send.at[t], rs_recv.at[t], {"gx": t}).wait_recv())
    summed[my_rows] = jnp.sum(pieces[...], axis=0) * scale
    out_copy = remote(summed.at[my_rows], summed.at[my_rows], core_sems.at[2], core_sems.at[3], {"gy": other})
    out_copy.start()

    fy_copy.wait_send()
    for exchange in halves:
        exchange.wait_send()

    def sent(j):
        fx_copy(j).wait_send()
        block_copy(j).wait_send()

    loop(1, n_gx, lambda s: sent(lax.rem(gx + s, n_gx)))
    others(lambda t: piece_copy(t).wait_send())
    gram_copy.wait_send()
    remote(summed.at[my_rows], summed.at[other_rows], core_sems.at[2], core_sems.at[3], {"gy": other}).wait_recv()
    third = summed[2 * side :]
    upper = jnp.concatenate([
        summed[: 2 * side], third, pltpu.roll(third, 2 * side, 1), pltpu.roll(summed[side : 2 * side], depth - side, 1)
    ], axis=0)
    row_block = lax.broadcasted_iota(jnp.int32, (depth, depth), 0) // side
    lane_block = lax.broadcasted_iota(jnp.int32, (depth, depth), 1) // side
    out_ref[...] = jnp.where(row_block > lane_block, upper.T, upper)
    out_copy.wait_send()


def solution(mesh):
    n_gx = mesh.shape["gx"]
    assert mesh.shape["gy"] == CORES

    def local(snapshot, factor_x, factor_y, factor_var):
        local_x, local_y, n_var, depth = snapshot.shape
        n_q = factor_var.shape[1]
        half_p = factor_y.shape[1]
        rank = factor_x.shape[1]
        k = half_p * n_q // n_gx
        scale = 1.0 / (rank * half_p * CORES * n_q)
        f32 = jnp.float32
        block = (n_gx, local_x, k, depth)
        packed = depth * 5 // 8
        dma = pltpu.SemaphoreType.DMA
        return pl.pallas_call(
            functools.partial(kernel, n_gx, scale),
            out_shape=jax.ShapeDtypeStruct((depth, depth), f32),
            in_specs=[
                pl.BlockSpec(memory_space=pltpu.HBM),
                pl.BlockSpec(memory_space=pltpu.HBM),
                pl.BlockSpec(memory_space=pltpu.HBM),
                pl.BlockSpec(memory_space=pltpu.HBM),
            ],
            out_specs=pl.BlockSpec(memory_space=pltpu.VMEM),
            scratch_shapes=[
                pltpu.VMEM(factor_x.shape, f32),
                pltpu.VMEM((half_p, local_y * CORES), f32),
                pltpu.SMEM((n_q, n_var), f32),
                pltpu.VMEM((local_x, n_var, local_y, depth), f32),
                pltpu.VMEM((n_q, local_y, local_x * depth), f32),
                pltpu.VMEM((n_gx, local_x, 1, depth), f32),
                pltpu.VMEM((half_p, local_y), f32),
                pltpu.VMEM(block, f32),
                pltpu.VMEM(block, f32),
                pltpu.VMEM(block, f32),
                pltpu.VMEM(block, f32),
                pltpu.VMEM((packed, depth), f32),
                pltpu.VMEM((packed // CORES, depth), f32),
                pltpu.VMEM((n_gx, packed // CORES, depth), f32),
                pltpu.VMEM((packed, depth), f32),
                dma((3,)), dma((local_x * CHUNKS,)), dma((2,)),
                dma((n_gx,)), dma((n_gx,)),
                dma((n_q,)), dma((n_q,)),
                dma((n_gx,)), dma((n_gx,)),
                dma((n_gx,)), dma((n_gx,)),
                dma((4,)),
            ],
            compiler_params=pltpu.CompilerParams(
                collective_id=0, has_side_effects=True, vmem_limit_bytes=24 * 1024 * 1024
            ),
        )(*[pltpu.with_memory_space_constraint(a, pltpu.HBM) for a in (jnp.transpose(snapshot, (0, 2, 1, 3)), factor_x, factor_y.T, factor_var.T)])

    in_specs = (P(("snap", "gx"), "gy", None, None), P("gx", None), P(None, "gy"), P())
    return jax.shard_map(local, mesh=mesh, in_specs=in_specs, out_specs=P("snap", None), check_vma=False)
```

```python
import functools

import jax
import jax.numpy as jnp
from jax import lax
from jax.experimental import pallas as pl
from jax.experimental.pallas import tpu as pltpu
from jax.sharding import PartitionSpec as P

MESH = pl.DeviceIdType.MESH
HIGHEST = lax.Precision.HIGHEST
CORES = 2
CHUNKS = 4


def dot(a, b, dims=((1,), (0,))):
    return lax.dot_general(a, b, (dims, ((), ())), precision=HIGHEST, preferred_element_type=jnp.float32)


def dot3(a, b, dims=((1,), (0,))):
    def part(x, y):
        return lax.dot_general(x, y, (dims, ((), ())), preferred_element_type=jnp.float32)

    a_high, b_high = a.astype(jnp.bfloat16), b.astype(jnp.bfloat16)
    a_low = (a - a_high.astype(jnp.float32)).astype(jnp.bfloat16)
    b_low = (b - b_high.astype(jnp.float32)).astype(jnp.bfloat16)
    return part(a_high, b_high) + (part(a_high, b_low) + part(a_low, b_high))


def loop(first, last, body):
    def step(i, carry):
        body(i)
        return carry

    lax.fori_loop(first, last, step, 0, unroll=(last - first) <= 16)


def kernel(
    n_gx, scale,
    snap_in, fx_in, fyt_in, fv_in, out_ref,
    fx_ref, fyt_ref, fv_ref, snap, reduced, fx_all, fy_recv, half_send, half_recv, part, blocks, gram, gram_recv, pieces, summed,
    in_sems, snap_sem, fy_sems, fx_send, fx_recv, half_ssem, half_rsem, a2a_send, a2a_recv, rs_send, rs_recv, core_sems, gram_sems,
):
    gx, gy = lax.axis_index("gx"), lax.axis_index("gy")
    other = 1 - gy
    local_x, n_var, local_y, depth = snap.shape
    n_q = reduced.shape[0]
    _, _, k, _ = blocks.shape
    per_q = n_gx // n_q
    half_rows = depth * 5 // 8 // CORES

    def remote(src, dst, send, recv, where):
        return pltpu.make_async_remote_copy(
            src_ref=src, dst_ref=dst, send_sem=send, recv_sem=recv, device_id=where, device_id_type=MESH
        )

    small = [
        pltpu.make_async_copy(src, dst, in_sems.at[i])
        for i, (src, dst) in enumerate(((fyt_in, fyt_ref), (fx_in, fx_ref), (fv_in, fv_ref)))
    ]
    for load in small:
        load.start()
    chunk = local_y // CHUNKS
    loads = []
    for x in range(local_x):
        for i in range(CHUNKS):
            at = pl.ds(i * chunk, chunk)
            loads.append(pltpu.make_async_copy(snap_in.at[x, :, at], snap.at[x, :, at], snap_sem.at[x * CHUNKS + i]))
    for load in loads:
        load.start()

    barrier = pltpu.get_barrier_semaphore()
    pl.semaphore_signal(barrier, inc=1, device_id={"gy": other}, device_id_type=MESH)
    loop(1, n_gx, lambda s: pl.semaphore_signal(
        barrier, inc=1, device_id={"gx": lax.rem(gx + s, n_gx)}, device_id_type=MESH))

    pl.semaphore_wait(barrier, n_gx)
    other_y = pl.ds(pl.multiple_of(other * local_y, local_y), local_y)
    fy_copy = remote(fyt_in.at[:, other_y], fy_recv, fy_sems.at[0], fy_sems.at[1], {"gy": other})
    fy_copy.start()
    for load in small:
        load.wait()
    fx = fx_ref[...]
    rank = fx.shape[1]
    fx_wide = jnp.concatenate([fx, jnp.zeros((local_x, depth - rank), jnp.float32)], axis=1) if rank < depth else fx
    for x in range(local_x):
        fx_all[gx, x] = fx_wide[x : x + 1]
    fy_mine = fyt_ref[:, pl.ds(pl.multiple_of(gy * local_y, local_y), local_y)]

    def fx_copy(j):
        return remote(fx_all.at[gx], fx_all.at[gx], fx_send.at[j], fx_recv.at[gx], {"gx": j})

    loop(1, n_gx, lambda s: fx_copy(lax.rem(gx + s, n_gx)).start())

    rows = 32
    for part_of, load in enumerate(loads):
        x, first = part_of // CHUNKS, part_of % CHUNKS * chunk
        load.wait()

        def var_step(i, carry, x=x, first=first):
            at = pl.ds(pl.multiple_of(first + i * rows, rows), rows)
            sums = [None] * n_q
            for v in range(n_var):
                cells = snap[x, v, at, :]
                for q in range(n_q):
                    term = cells * fv_ref[q, v]
                    sums[q] = term if v == 0 else sums[q] + term
            for q in range(n_q):
                reduced[q, at, x * depth : (x + 1) * depth] = sums[q]
            return carry

        lax.fori_loop(0, chunk // rows, var_step, 0)

    def put(ref, q, value):
        for x in range(local_x):
            cells = value[:, x * depth : (x + 1) * depth]
            ref[pl.ds(q * per_q, per_q), x] = cells.reshape(per_q, k, depth)

    fy_copy.wait_recv()
    fy_both = jnp.concatenate([fy_recv[...], fy_mine], axis=0)
    half_p = fy_recv.shape[0]
    halves = []
    for q in range(n_q):
        both = dot(fy_both, reduced[q])
        put(half_send, q, both[:half_p])
        put(part, q, both[half_p:])
        at = pl.ds(q * per_q, per_q)
        exchange = remote(half_send.at[at], half_recv.at[at], half_ssem.at[q], half_rsem.at[q], {"gy": other})
        exchange.start()
        halves.append(exchange)

    def block_copy(j):
        return remote(part.at[j], blocks.at[gx], a2a_send.at[j], a2a_recv.at[gx], {"gx": j})

    for q, exchange in enumerate(halves):
        at = pl.ds(q * per_q, per_q)
        exchange.wait_recv()
        part[at] = part[at] + half_recv[at]

        def send_block(j):
            @pl.when(j != gx)
            def _():
                block_copy(j).start()

        loop(0, per_q, lambda i, q=q: send_block(q * per_q + i))
    blocks[gx] = part[gx]

    def arrived(sems, ref, j):
        remote(ref.at[gx], ref.at[j], fx_send.at[j], sems.at[j], {"gx": j}).wait_recv()

    loop(1, n_gx, lambda s: arrived(fx_recv, fx_all, lax.rem(gx + s, n_gx)))
    wide = n_gx * local_x * k
    factor = jnp.broadcast_to(fx_all[...], (n_gx, local_x, k, depth)).reshape(wide, depth)
    largest = jnp.max(jnp.abs(factor), axis=1, keepdims=True)
    largest = jnp.where(largest > 0.0, largest, 1.0)
    unit = factor / largest
    same = (
        lax.broadcasted_iota(jnp.int32, (wide, wide), 0) % k
        == lax.broadcasted_iota(jnp.int32, (wide, wide), 1) % k
    )
    mixing = jnp.where(same, dot(unit, unit, ((1,), (1,))), 0.0)

    loop(1, n_gx, lambda s: arrived(a2a_recv, blocks, lax.rem(gx + s, n_gx)))
    cells = blocks[...].reshape(wide, depth) * largest
    square = dot3(cells, dot3(mixing, cells), ((0,), (0,)))
    side = depth // 4
    lane = lax.broadcasted_iota(jnp.int32, (side, depth), 1)
    gram[:side] = square[:side]
    gram[side : 2 * side] = jnp.where(lane < side, pltpu.roll(square[3 * side :], side, 1), square[side : 2 * side])
    third, split = square[2 * side : 3 * side], side // 2
    gram[2 * side :] = jnp.where(lane[:split] < 2 * side, pltpu.roll(third[split:], 2 * side, 1), third[:split])

    def others(body):
        loop(1, n_gx, lambda s: body(lax.rem(gx + s, n_gx)))

    my_rows = pl.ds(pl.multiple_of(gy * half_rows, 8), half_rows)
    other_rows = pl.ds(pl.multiple_of(other * half_rows, 8), half_rows)
    first = half_rows // 16 * 8
    spans = ((0, first), (first, half_rows - first))

    def gram_copy(i):
        at, size = spans[i]
        theirs = pl.ds(pl.multiple_of(other * half_rows + at, 8), size)
        return remote(gram.at[theirs], gram_recv.at[pl.ds(at, size)], gram_sems.at[i], gram_sems.at[2 + i], {"gy": other})

    def piece_copy(i, t, source):
        at = pl.ds(*spans[i])
        return remote(pieces.at[gx, at], pieces.at[source, at], rs_send.at[i, t], rs_recv.at[i, source], {"gx": t})

    for i in range(2):
        gram_copy(i).start()
    for i, (at, size) in enumerate(spans):
        gram_copy(i).wait_recv()
        mine = pl.ds(pl.multiple_of(gy * half_rows + at, 8), size)
        pieces[gx, pl.ds(at, size)] = gram[mine] + gram_recv[pl.ds(at, size)]
        others(lambda t, i=i: piece_copy(i, t, gx).start())
    for i in range(2):
        others(lambda t, i=i: piece_copy(i, t, t).wait_recv())
    summed[my_rows] = jnp.sum(pieces[...], axis=0) * scale
    out_copy = remote(summed.at[my_rows], summed.at[my_rows], core_sems.at[2], core_sems.at[3], {"gy": other})
    out_copy.start()

    fy_copy.wait_send()
    for exchange in halves:
        exchange.wait_send()

    def sent(j):
        fx_copy(j).wait_send()
        block_copy(j).wait_send()

    loop(1, n_gx, lambda s: sent(lax.rem(gx + s, n_gx)))
    for i in range(2):
        others(lambda t, i=i: piece_copy(i, t, gx).wait_send())
        gram_copy(i).wait_send()
    remote(summed.at[my_rows], summed.at[other_rows], core_sems.at[2], core_sems.at[3], {"gy": other}).wait_recv()
    third = summed[2 * side :]
    upper = jnp.concatenate([
        summed[: 2 * side], third, pltpu.roll(third, 2 * side, 1), pltpu.roll(summed[side : 2 * side], depth - side, 1)
    ], axis=0)
    row_block = lax.broadcasted_iota(jnp.int32, (depth, depth), 0) // side
    lane_block = lax.broadcasted_iota(jnp.int32, (depth, depth), 1) // side
    out_ref[...] = jnp.where(row_block > lane_block, upper.T, upper)
    out_copy.wait_send()


def solution(mesh):
    n_gx = mesh.shape["gx"]
    assert mesh.shape["gy"] == CORES

    def local(snapshot, factor_x, factor_y, factor_var):
        local_x, local_y, n_var, depth = snapshot.shape
        n_q = factor_var.shape[1]
        half_p = factor_y.shape[1]
        rank = factor_x.shape[1]
        k = half_p * n_q // n_gx
        scale = 1.0 / (rank * half_p * CORES * n_q)
        f32 = jnp.float32
        block = (n_gx, local_x, k, depth)
        packed = depth * 5 // 8
        dma = pltpu.SemaphoreType.DMA
        return pl.pallas_call(
            functools.partial(kernel, n_gx, scale),
            out_shape=jax.ShapeDtypeStruct((depth, depth), f32),
            in_specs=[
                pl.BlockSpec(memory_space=pltpu.HBM),
                pl.BlockSpec(memory_space=pltpu.HBM),
                pl.BlockSpec(memory_space=pltpu.HBM),
                pl.BlockSpec(memory_space=pltpu.HBM),
            ],
            out_specs=pl.BlockSpec(memory_space=pltpu.VMEM),
            scratch_shapes=[
                pltpu.VMEM(factor_x.shape, f32),
                pltpu.VMEM((half_p, local_y * CORES), f32),
                pltpu.SMEM((n_q, n_var), f32),
                pltpu.VMEM((local_x, n_var, local_y, depth), f32),
                pltpu.VMEM((n_q, local_y, local_x * depth), f32),
                pltpu.VMEM((n_gx, local_x, 1, depth), f32),
                pltpu.VMEM((half_p, local_y), f32),
                pltpu.VMEM(block, f32),
                pltpu.VMEM(block, f32),
                pltpu.VMEM(block, f32),
                pltpu.VMEM(block, f32),
                pltpu.VMEM((packed, depth), f32),
                pltpu.VMEM((packed // CORES, depth), f32),
                pltpu.VMEM((n_gx, packed // CORES, depth), f32),
                pltpu.VMEM((packed, depth), f32),
                dma((3,)), dma((local_x * CHUNKS,)), dma((2,)),
                dma((n_gx,)), dma((n_gx,)),
                dma((n_q,)), dma((n_q,)),
                dma((n_gx,)), dma((n_gx,)),
                dma((2, n_gx)), dma((2, n_gx)),
                dma((4,)), dma((4,)),
            ],
            compiler_params=pltpu.CompilerParams(
                collective_id=0, has_side_effects=True, vmem_limit_bytes=24 * 1024 * 1024
            ),
        )(*[pltpu.with_memory_space_constraint(a, pltpu.HBM) for a in (jnp.transpose(snapshot, (0, 2, 1, 3)), factor_x, factor_y.T, factor_var.T)])

    in_specs = (P(("snap", "gx"), "gy", None, None), P("gx", None), P(None, "gy"), P())
    return jax.shard_map(local, mesh=mesh, in_specs=in_specs, out_specs=P("snap", None), check_vma=False)
```
